256 devices in a mesh: inst: 16 (over z, x_hi), tp: 16 (over x_lo, y, core).
Axes of the slice: x: 4 (x_hi: 2, x_lo: 2; x = x_hi * 2 + x_lo), y: 4, z: 8, core: 2. Of those that a mesh axis runs over, the one named last changes fastest.
Arguments:
- tokens: bfloat16 [16384, 4608], P(('inst', 'tp')), may hold values from -6 to 6
- w_query: bfloat16 [4608, 4096], P(None, 'tp'), may hold values from -0.09375 to 0.09375
- w_keyval: bfloat16 [4608, 4096], P(None, 'tp'), may hold values from -0.09375 to 0.09375
- w_out: bfloat16 [4096, 4608], P('tp'), may hold values from -0.09375 to 0.09375
- kv_pool: bfloat16 [512, 256, 4096], P('inst', None, 'tp'), may hold values from -6 to 6
- req_target: int32 [16, 16], P('inst'), may hold values from 0 to 15, each once within a row
- page_counts: int32 [16, 16], P('inst'), may hold values from 1 to 4, 32 in all within a row
- tail_tokens: int32 [16, 16], P('inst'), may hold values from 1 to 256
- migrate: int32 [16, 16], P('inst'), may hold values 0 or 1
- pool_order: int32 [16, 32], P('inst'), may hold values from 0 to 31, each once within a row
Outputs:
- attn_out: bfloat16 [16384, 4608], P(('inst', 'tp'))
The draws below stay inside these ranges and needn't reach their ends.
Inputs may be any that keep to these rules, and one draw needn't show every extreme that they name: `req_target`: each row is a permutation: every source sends exactly one request to every target instance. `page_counts`: each source's requests hold all of its 32 pages together, and some request of every source holds 4 pages. `pool_order`: each row is a permutation of the source's pages.
All inputs are finite; a program needn't handle non-finite values. No bound on the sum of `migrate` on one device may be relied on, other than what follows from the above.
Results may differ from the reference program's by a relative error of at most 0.023.
Values may be sent and summed in bfloat16 or wider, within the bound.
A program may use at most 128 MiB of HBM per device.

```python
import math
import jax
import jax.numpy as jnp
import numpy as np
from jax import lax

D = 4608
HEADS = 32
KV_HEADS = 16
HD = 128
QR = 64
PAGE = 256
PPR = 4
POOL = 32
ROWS = 16384
N_INST = 16
N_TP = 16


def plant(drawn, stream_key, least, largest):
    longest = drawn.shape.index(max(drawn.shape))
    spots = []
    for shift in (0, 1):
        where = [jax.random.randint(jax.random.fold_in(stream_key, axis), (), 0, length) for axis, length in enumerate(drawn.shape)]
        where[longest] = (where[longest] + shift) % drawn.shape[longest]
        spots.append(tuple(where))
    return drawn.at[spots[0]].set(least).at[spots[1]].set(largest)


def shard_levels(key, dims, cuts, low, high):
    def one(position, parts):
        steps = jax.random.uniform(jax.random.fold_in(jax.random.fold_in(key, 6), position), (parts,), jnp.float32, low / len(cuts), high / len(cuts))
        return jnp.repeat(jnp.exp(steps), dims[position] // parts).reshape((-1,) + (1,) * (len(dims) - position - 1))

    factor_of = one(*cuts[0])
    for cut in cuts[1:]:
        factor_of = factor_of * one(*cut)
    return factor_of


def split_up(amount, total, most, skew):
    loads = [(1 << 20) // math.isqrt(rank ** skew) + 1 for rank in range(2, amount + 1)]
    rest, given = total - most - (amount - 1), [1] * (amount - 1)
    while rest > 0:
        candidates = [i for i in range(amount - 1) if given[i] < most]
        mass, left = sum([loads[i] for i in candidates]), rest
        for i in candidates:
            more = min(most - given[i], max(1, left * loads[i] // mass), rest)
            given[i] = given[i] + more
            rest = rest - more
    return np.array([most] + given)


def uneven(rng, count, total, limit, slope):
    if count == 2:
        one = jax.random.randint(rng, (), max(1, total - limit), min(limit, total - 1) + 1)
        return jnp.stack([one, total - one])
    lengths = jnp.asarray(split_up(count, total, limit, slope), jnp.int32)
    couples = (count - 1) // 2
    donor, receiver = lengths[1:1 + 2 * couples:2], lengths[2:2 + 2 * couples:2]
    margin = jnp.minimum(donor - 1, limit - receiver)
    moved = jax.random.randint(jax.random.fold_in(rng, 1), (couples,), 0, 1 << 20) % (margin + 1)
    lengths = lengths.at[1:1 + 2 * couples:2].set(donor - moved).at[2:2 + 2 * couples:2].set(receiver + moved)
    return lengths[jax.random.permutation(jax.random.fold_in(rng, 2), count)]


def normal_values(rng, extent, deviation, limit, shards=(), kind=jnp.bfloat16):
    values = jax.random.normal(rng, extent, jnp.float32) * deviation
    if len(shards) > 0:
        values = shard_levels(rng, extent, shards, -0.22, 0.18) * values
    return jnp.clip(values, min=-limit, max=limit).astype(kind)


def setup_inputs(seed: int = 0) -> dict:
    key_list = jax.random.split(jax.random.key(seed), 11)
    return {
        "tokens": normal_values(key_list[0], (ROWS, D), 1.0, 6.0, ((0, 256),)),
        "w_query": normal_values(key_list[1], (D, HEADS * HD), D ** -0.5, 0.09375, ((1, 16),)),
        "w_keyval": normal_values(key_list[2], (D, KV_HEADS * 2 * HD), D ** -0.5, 0.09375, ((1, 16),)),
        "w_out": normal_values(key_list[3], (HEADS * HD, D), (HEADS * HD) ** -0.5, 0.09375, ((0, 16),)),
        "kv_pool": normal_values(key_list[4], (N_INST * POOL, PAGE, KV_HEADS * 2 * HD), 1.0, 6.0, ((0, 16), (2, 16))),
        "req_target": jax.vmap(lambda own: jax.random.permutation(own, N_INST))(jax.random.split(key_list[5], N_INST)).reshape((N_INST, N_INST)).astype(jnp.int32),
        "page_counts": jax.vmap(lambda own: uneven(own, N_INST, POOL, PPR, 2))(jax.random.split(key_list[6], N_INST)).reshape((N_INST, N_INST)).astype(jnp.int32),
        "tail_tokens": plant(jax.random.randint(key_list[7], (N_INST, N_INST), 1, PAGE + 1), jax.random.fold_in(key_list[7], 1), 1, PAGE).astype(jnp.int32),
        "migrate": plant((jax.random.randint(key_list[8], (N_INST, N_INST), 0, 8) < 7).astype(jnp.int32), jax.random.fold_in(key_list[8], 1), 0, 1),
        "pool_order": jax.vmap(lambda own: jax.random.permutation(own, POOL))(jax.random.split(key_list[9], N_INST)).reshape((N_INST, POOL)).astype(jnp.int32),
    }


SOFTCAP = 50.0
ROPE_BASE = 10000.0


def rounded(values):
    return lax.optimization_barrier(values.astype(jnp.bfloat16)).astype(jnp.float32)


def rotate(vectors, positions):
    head_dim = vectors.shape[-1]
    half_dim = head_dim // 2
    frequency = ROPE_BASE ** (-2.0 * jnp.arange(half_dim, dtype=jnp.float32) / head_dim)
    angles = positions.astype(jnp.float32)[:, None] * frequency[None, :]
    cosine = jnp.cos(angles)[:, None, :]
    sines = jnp.sin(angles)[:, None, :]
    leading = vectors[..., :half_dim]
    trailing = vectors[..., half_dim:]
    return jnp.concatenate([leading * cosine - trailing * sines, trailing * cosine + leading * sines], axis=-1)


def capped_weights(scores):
    return jnp.exp(SOFTCAP * jnp.tanh(scores / SOFTCAP) - SOFTCAP)


def source_tables(targets, counts, tail_len, flag_set, pool_order):
    number = targets.shape[0]
    matches = (targets[:, None] == jnp.arange(number, dtype=jnp.int32)[None, :]).astype(jnp.int32)
    starts = (jnp.cumsum(counts) - counts).astype(jnp.int32)

    def pick(column):
        return jnp.sum(column[:, None] * matches, axis=0).astype(jnp.int32)

    count_to = pick(counts)
    cached = pick(flag_set) * ((count_to - 1) * PAGE + pick(tail_len))
    slots = pick(starts)[:, None] + jnp.arange(PPR, dtype=jnp.int32)[None, :]
    slots = jnp.minimum(slots, pool_order.shape[0] - 1)
    return cached.astype(jnp.int32), pool_order[slots]


def block_part(queries, keys, values, score_scale):
    scores = jnp.einsum("nihgd,njhd->nhgij", queries, keys) * score_scale
    length = queries.shape[1]
    causal = jnp.arange(length)[:, None] >= jnp.arange(length)[None, :]
    softmax_w = jnp.where(causal, capped_weights(scores), 0.0)
    totals = jnp.transpose(jnp.sum(softmax_w, axis=-1), (0, 3, 1, 2))
    weighted = jnp.einsum("nhgij,njhd->nihgd", rounded(softmax_w), values)
    return totals, weighted


def cache_part(queries, cache_pages, cached, score_scale):
    shape_in = cache_pages.shape
    heads = queries.shape[2]
    head_dim = queries.shape[4]
    stacked = cache_pages.astype(jnp.float32).reshape(shape_in[0], shape_in[1] * shape_in[2], heads, 2, head_dim)
    keys = stacked[:, :, :, 0]
    values = stacked[:, :, :, 1]
    scores = jnp.einsum("nihgd,nchd->nhgic", queries, keys) * score_scale
    live_mask = jnp.arange(keys.shape[1])[None, :] < cached[:, None]
    softmax_w = jnp.where(live_mask[:, None, None, None, :], capped_weights(scores), 0.0)
    totals = jnp.transpose(jnp.sum(softmax_w, axis=-1), (0, 3, 1, 2))
    weighted = jnp.einsum("nhgic,nchd->nihgd", rounded(softmax_w), values)
    return totals, weighted


def reference(tokens, w_query, w_keyval, w_out, kv_pool, req_target, page_counts, tail_tokens, migrate, pool_order):
    cached_all, ids_all = jax.vmap(source_tables)(req_target, page_counts, tail_tokens, migrate, pool_order)
    row_count = N_INST * QR
    groups = HEADS // KV_HEADS
    score_scale = (D // HEADS) ** -0.5
    group_width = HEADS * HD // N_TP
    pool_base = (jnp.arange(N_INST, dtype=jnp.int32) * POOL)[:, None]

    def one_target(target):
        block_in = lax.dynamic_slice_in_dim(tokens, target * row_count, row_count, 0)
        cached = lax.dynamic_index_in_dim(cached_all, target, 1, keepdims=False)
        page_ids = lax.dynamic_index_in_dim(ids_all, target, 1, keepdims=False) + pool_base
        positions = (cached[:, None] + jnp.arange(QR, dtype=jnp.int32)[None, :]).reshape(row_count)
        projected_q = jnp.dot(block_in, w_query, preferred_element_type=jnp.float32)
        projected_kv = jnp.dot(block_in, w_keyval, preferred_element_type=jnp.float32)
        queries = rounded(rotate(projected_q.reshape(row_count, HEADS, HD), positions))
        keyval = projected_kv.reshape(row_count, KV_HEADS, 2, HD)
        keys = rounded(rotate(keyval[:, :, 0], positions))
        values = rounded(keyval[:, :, 1])
        queries = queries.reshape(N_INST, QR, KV_HEADS, groups, HD)
        keys = keys.reshape(N_INST, QR, KV_HEADS, HD)
        values = values.reshape(N_INST, QR, KV_HEADS, HD)
        totals, weighted = block_part(queries, keys, values, score_scale)
        far_totals, far_weighted = cache_part(queries, kv_pool[page_ids], cached, score_scale)
        attended = ((weighted + far_weighted) / (totals + far_totals)[..., None]).astype(jnp.bfloat16)
        attended = attended.reshape(row_count, N_TP, group_width).astype(jnp.float32)
        weights_out = w_out.reshape(N_TP, group_width, D).astype(jnp.float32)
        partial_out = jnp.einsum("rpw,pwd->prd", attended, weights_out)
        return jnp.sum(rounded(partial_out), axis=0).astype(jnp.bfloat16)

    outputs = lax.map(one_target, jnp.arange(N_INST, dtype=jnp.int32))
    return outputs.reshape(N_INST * row_count, D)
```

```python
import jax
import jax.numpy as jnp
from jax import lax
from jax.sharding import PartitionSpec as P

D = 4608
HEADS = 32
HD = 128
PAGE = 256
PPR = 4


SOFTCAP = 50.0
ROPE_BASE = 10000.0


def rotate(vectors, positions):
    head_dim = vectors.shape[-1]
    half_dim = head_dim // 2
    frequency = ROPE_BASE ** (-2.0 * jnp.arange(half_dim, dtype=jnp.float32) / head_dim)
    angles = positions.astype(jnp.float32)[:, None] * frequency[None, :]
    cosine = jnp.cos(angles)[:, None, :]
    sines = jnp.sin(angles)[:, None, :]
    leading = vectors[..., :half_dim]
    trailing = vectors[..., half_dim:]
    return jnp.concatenate(
        [leading * cosine - trailing * sines, trailing * cosine + leading * sines], axis=-1
    )


def capped_weights(scores):
    return jnp.exp(SOFTCAP * jnp.tanh(scores / SOFTCAP) - SOFTCAP)


def source_tables(targets, counts, tail_len, flag_set, pool_order):
    number = targets.shape[0]
    matches = (targets[:, None] == jnp.arange(number, dtype=jnp.int32)[None, :]).astype(jnp.int32)
    starts = jnp.cumsum(counts) - counts

    def pick(column):
        return jnp.sum(column[:, None] * matches, axis=0)

    count_to = pick(counts)
    cached = pick(flag_set) * ((count_to - 1) * PAGE + pick(tail_len))
    slots = pick(starts)[:, None] + jnp.arange(PPR, dtype=jnp.int32)[None, :]
    slots = jnp.minimum(slots, pool_order.shape[0] - 1)
    return (cached, pool_order[slots])


def block_part(queries, keys, values, score_scale):
    scores = (
        jnp.einsum("nihgd,njhd->nhgij", queries, keys, preferred_element_type=jnp.float32)
        * score_scale
    )
    length = queries.shape[1]
    causal = jnp.arange(length)[:, None] >= jnp.arange(length)[None, :]
    softmax_w = jnp.where(causal, capped_weights(scores), 0.0)
    totals = jnp.transpose(jnp.sum(softmax_w, axis=-1), (0, 3, 1, 2))
    weighted = jnp.einsum(
        "nhgij,njhd->nihgd",
        softmax_w.astype(jnp.bfloat16),
        values,
        preferred_element_type=jnp.float32,
    )
    return (totals, weighted)


def cache_part(queries, cache_pages, cached, score_scale):
    shape_in = cache_pages.shape
    heads = queries.shape[2]
    head_dim = queries.shape[4]
    stacked = cache_pages.reshape(shape_in[0], shape_in[1] * shape_in[2], heads, 2, head_dim)
    keys = stacked[:, :, :, 0]
    values = stacked[:, :, :, 1]
    scores = (
        jnp.einsum("nihgd,nchd->nhgic", queries, keys, preferred_element_type=jnp.float32)
        * score_scale
    )
    live_mask = jnp.arange(keys.shape[1])[None, :] < cached[:, None]
    softmax_w = jnp.where(live_mask[:, None, None, None, :], capped_weights(scores), 0.0)
    totals = jnp.transpose(jnp.sum(softmax_w, axis=-1), (0, 3, 1, 2))
    weighted = jnp.einsum(
        "nhgic,nchd->nihgd",
        softmax_w.astype(jnp.bfloat16),
        values,
        preferred_element_type=jnp.float32,
    )
    return (totals, weighted)


def shards(
    tokens,
    w_query,
    w_keyval,
    w_out,
    kv_pool,
    req_target,
    page_counts,
    tail_tokens,
    migrate,
    pool_order,
):
    instances = lax.axis_size("inst")
    query_width = w_query.shape[1]
    local_heads = w_keyval.shape[1] // (2 * HD)
    groups = query_width // (local_heads * HD)
    row_count = tokens.shape[0] * lax.axis_size("tp")
    per_request = row_count // instances
    score_scale = (D // HEADS) ** (-0.5)
    cached_out, page_ids = source_tables(
        req_target[0], page_counts[0], tail_tokens[0], migrate[0], pool_order[0]
    )
    near = jnp.tile(jnp.arange(per_request, dtype=jnp.int32), instances)
    piece = lax.all_gather(tokens, "tp", axis=0, tiled=True)
    projected = jnp.concatenate(
        [
            jnp.dot(piece, w_query, preferred_element_type=jnp.float32),
            jnp.dot(piece, w_keyval, preferred_element_type=jnp.float32),
        ],
        axis=1,
    )
    queries = rotate(
        projected[:, :query_width].reshape(row_count, local_heads * groups, HD), near
    ).astype(jnp.bfloat16)
    keyval = projected[:, query_width:].reshape(row_count, local_heads, 2, HD)
    keys = rotate(keyval[:, :, 0], near).astype(jnp.bfloat16)
    values = keyval[:, :, 1].astype(jnp.bfloat16)
    there = lax.all_to_all(
        queries.reshape(instances, per_request, query_width),
        "inst", split_axis=0, concat_axis=0, tiled=True,
    )
    offsets = jnp.repeat(cached_out, per_request)
    there = rotate(
        there.reshape(row_count, local_heads * groups, HD).astype(jnp.float32), offsets
    ).astype(jnp.bfloat16)
    there = there.reshape(instances, per_request, local_heads, groups, HD)
    far_totals, far_weighted = cache_part(there, kv_pool[page_ids], cached_out, score_scale)
    far_weighted = lax.all_to_all(
        far_weighted.astype(jnp.bfloat16).reshape(instances, per_request, query_width),
        "inst", split_axis=0, concat_axis=0, tiled=True,
    ).reshape(instances, per_request, local_heads, groups, HD).astype(jnp.float32)
    far_totals = lax.all_to_all(
        far_totals.reshape(instances, per_request * local_heads * groups),
        "inst", split_axis=0, concat_axis=0, tiled=True,
    ).reshape(instances, per_request, local_heads, groups)
    queries = queries.reshape(instances, per_request, local_heads, groups, HD)
    keys = keys.reshape(instances, per_request, local_heads, HD)
    values = values.reshape(instances, per_request, local_heads, HD)
    totals, weighted = block_part(queries, keys, values, score_scale)
    attended = ((weighted + far_weighted) / (totals + far_totals)[..., None]).astype(jnp.bfloat16)
    attended = attended.reshape(row_count, query_width)
    return lax.psum_scatter(
        jnp.dot(attended, w_out, preferred_element_type=jnp.float32).astype(jnp.bfloat16),
        "tp",
        scatter_dimension=0,
        tiled=True,
    )


def solution(mesh):
    return jax.shard_map(
        shards,
        mesh=mesh,
        in_specs=(
            P(("inst", "tp"), None),
            P(None, "tp"),
            P(None, "tp"),
            P("tp", None),
            P("inst", None, "tp"),
            P("inst", None),
            P("inst", None),
            P("inst", None),
            P("inst", None),
            P("inst", None),
        ),
        out_specs=P(("inst", "tp"), None),
        check_vma=False,
    )
```

```python
import math

import jax
import jax.numpy as jnp
import numpy as np
from jax import lax
from jax.experimental import pallas as pl
from jax.experimental.pallas import tpu as pltpu
from jax.sharding import PartitionSpec as P

D = 4608
HEADS = 32
HD = 128
QR = 64
HALF = QR // 2
PAGE = 256
POOL = 32
N = 16
SOFTCAP = 50.0
ROPE_BASE = 10000.0
COLS = 512
STEPS = D // COLS
MSG = 2 * QR
OMSG = MSG + 16
MESH = pl.DeviceIdType.MESH
F32 = jnp.float32
BF16 = jnp.bfloat16
SHARP = SOFTCAP * math.log2(math.e)


def tables():
    k = np.arange(HD // 2, dtype=np.float64)
    freq = (ROPE_BASE ** (-2.0 * k / HD)).astype(np.float32)
    angle = np.arange(QR, dtype=np.float64)[:, None] * freq.astype(np.float64)[None, :]
    cos = np.concatenate([np.cos(angle)] * 2, axis=1)
    sin = np.concatenate([-np.sin(angle), np.sin(angle)], axis=1)
    scale = (D // HEADS) ** -0.5 / SOFTCAP
    row = np.tile(np.concatenate([freq, freq])[None, :], (8, 1))
    return np.concatenate([cos * scale, sin * scale, cos, sin, row], axis=0).astype(np.float32)


def swap(i):
    return i + (i // 2) * (1 - 2 * (i % 2))


def turn(v, cos, sin):
    return v * cos + pltpu.roll(v, HD // 2, 1) * sin


def weights_of(scores):
    return jnp.exp2(SHARP * jnp.tanh(scores))


def dot_t(a, b):
    return lax.dot_general(a, b, (((1,), (1,)), ((), ())), preferred_element_type=F32)


def kernel(
    tok, wq_in, wkv_in, wo_in, pool_in, tgt, cnt, tail, mig, order, tab_in,
    out,
    xb, wq, wkv, wo, pool, tab, qout, qin, qrot, near_w, near_t, far_w, far_l, oout, oin, att,
    part, rx, ry, fin, turn_c, turn_s,
    cached_s, eslot, whose,
    sl, sw_s, sw_r, sy_s, sy_r, sx_s, sx_r, sq_s, sq_r, so_s, so_r, tx_s, tx_r, ty_s, ty_r,
):
    inst = lax.axis_index("inst")
    j = lax.axis_index("tp")
    z = inst // 2
    xh = inst % 2
    xl = j // 8
    y = (j // 2) % 4
    c = j % 2
    x = 2 * xh + xl

    def dev(px, py, pz, pc):
        return (pz * 2 + px // 2, (px % 2) * 8 + py * 2 + pc)

    up, down = (y + 1) % 4, (y + 3) % 4
    fx = (x + 1 + 2 * c) % 4
    bx = (x + 3 + 2 * c) % 4
    y_up, y_down = dev(x, up, z, c), dev(x, down, z, c)
    x_fwd, x_back = dev(fx, y, z, c), dev(bx, y, z, c)
    mate = dev(x, y, z, 1 - c)

    def remote(src, dst, ss, rs, to):
        return pltpu.make_async_remote_copy(
            src_ref=src, dst_ref=dst, send_sem=ss, recv_sem=rs, device_id=to, device_id_type=MESH
        )

    local = [
        pltpu.make_async_copy(tok, xb.at[pl.ds(0, QR)], sl.at[0]),
        pltpu.make_async_copy(wq_in, wq.at[c], sl.at[1]),
        pltpu.make_async_copy(wkv_in, wkv.at[c], sl.at[2]),
        pltpu.make_async_copy(tab_in, tab, sl.at[3]),
        pltpu.make_async_copy(wo_in, wo.at[pl.ds(pl.multiple_of(c * 256, 256), 256)], sl.at[4]),
        pltpu.make_async_copy(pool_in, pool, sl.at[5]),
    ]
    for copy in local:
        copy.start()

    barrier = pltpu.get_barrier_semaphore()
    for to in (y_up, y_down, x_fwd, x_back):
        pl.semaphore_signal(barrier, inc=1, device_id=to, device_id_type=MESH)

    def greet(i, carry):
        to = ((i // 4) * 2 + (i // 2) % 2, xl * 8 + y * 2 + i % 2)

        @pl.when((to[0] != inst) | (to[1] != j))
        def _():
            pl.semaphore_signal(barrier, inc=1, device_id=to, device_id_type=MESH)

        return carry

    lax.fori_loop(0, 32, greet, 0)
    pl.semaphore_wait(barrier, 35)

    def rows(k, half=None):
        if half is None:
            return pl.ds(k * QR, QR)
        return pl.ds(k * QR + half * HALF, HALF)

    def tok_half(half):
        return tok.at[pl.ds(half * HALF, HALF)]

    y_copies = [
        remote(tok_half(0), xb.at[rows(4, 0)], sy_s.at[0], sy_r.at[0], y_up),
        remote(tok_half(1), xb.at[rows(2, 1)], sy_s.at[1], sy_r.at[1], y_down),
        remote(tok_half(1), xb.at[rows(4, 1)], sy_s.at[2], sy_r.at[2], y_up),
        remote(tok_half(0), xb.at[rows(2, 0)], sy_s.at[3], sy_r.at[3], y_down),
        remote(xb.at[rows(4, 0)], xb.at[rows(6, 0)], sy_s.at[4], sy_r.at[4], y_up),
        remote(xb.at[rows(2, 1)], xb.at[rows(6, 1)], sy_s.at[5], sy_r.at[5], y_down),
    ]

    def x_copy(i, k, half):
        return remote(xb.at[rows(k, half)], xb.at[rows(k + 1, half)], sx_s.at[i], sx_r.at[i], x_fwd)

    x_copies = [
        remote(tok, xb.at[rows(1)], sx_s.at[0], sx_r.at[0], x_fwd),
        x_copy(1, 4, 0), x_copy(2, 2, 1), x_copy(3, 4, 1), x_copy(4, 2, 0), x_copy(5, 6, 0), x_copy(6, 6, 1),
    ]
    w_copies = [
        remote(wq_in, wq.at[c], sw_s.at[0], sw_r.at[0], mate),
        remote(wkv_in, wkv.at[c], sw_s.at[1], sw_r.at[1], mate),
        remote(wo_in, wo.at[pl.ds(pl.multiple_of(c * 256, 256), 256)], sw_s.at[2], sw_r.at[2], mate),
    ]

    def w_arrive(i, ref):
        pltpu.make_async_copy(ref, ref, sw_r.at[i]).wait()

    y_copies[0].start()
    y_copies[1].start()
    x_copies[0].start()
    y_copies[2].start()
    y_copies[3].start()
    w_copies[0].start()
    w_copies[1].start()
    w_copies[2].start()

    local[3].wait()
    freq = tab[pl.ds(4 * QR, 8), :]
    sign = jnp.where(lax.broadcasted_iota(jnp.int32, (8, HD), 1) < HD // 2, -1.0, 1.0)

    def request(r, end):
        cached = mig[0, r] * ((cnt[0, r] - 1) * PAGE + tail[0, r])
        cached_s[r] = cached
        angle = cached.astype(F32) * freq
        turn_c[r] = jnp.cos(angle)
        turn_s[r] = jnp.sin(angle) * sign
        return end

    lax.fori_loop(0, N, request, 0)

    def ends(t, carry):
        def one(r, state):
            end, found, who = state
            end = end + cnt[0, r]
            hit = tgt[0, r] == t
            return end, jnp.where(hit, end, found), jnp.where(hit, r, who)

        state = lax.fori_loop(0, N, one, (jnp.int32(0), jnp.int32(0), jnp.int32(0)))
        eslot[t] = state[1]
        whose[t] = state[2]
        return carry

    lax.fori_loop(0, N, ends, 0)

    def q_route(k, e):
        group, cross = k // 2, k % 2
        offset = swap(group)
        ox = x + cross * (bx - x)
        oy = (y + offset) % 4
        zs = (ox % 2) * 4 + oy
        here = (zs == z) & (xh == c) & (e == c)
        return here, dev(2 * c + xl, y, zs, e), z * 2 + ox // 2

    def q_copy(k, e, to, t):
        return remote(qout.at[k, e], qin.at[t], sq_s.at[k * 2 + e], sq_r.at[t], to)

    def q_send(k, e):
        here, to, t = q_route(k, e)

        @pl.when(here)
        def _():
            own = pltpu.make_async_copy(qout.at[k, e], qin.at[t], sl.at[6])
            own.start()
            own.wait()

        @pl.when(jnp.logical_not(here))
        def _():
            q_copy(k, e, to, t).start()

    causal = (
        lax.broadcasted_iota(jnp.int32, (MSG, QR), 0) % QR
        >= lax.broadcasted_iota(jnp.int32, (MSG, QR), 1)
    )

    def handle(k0, nb):
        span = pl.ds(k0 * QR, nb * QR)

        def per_core(e, carry):
            cq, sq = tab[pl.ds(0, QR), :], tab[pl.ds(QR, QR), :]
            q = jnp.dot(xb[span, :], wq[e], preferred_element_type=F32)
            for b in range(nb):
                for h in range(2):
                    v = q[b * QR:(b + 1) * QR, h * HD:(h + 1) * HD]
                    qout[k0 + b, e, pl.ds(h * QR, QR), :] = turn(v, cq, sq).astype(BF16)
            return carry

        def near(e, carry):
            ck, sk = tab[pl.ds(2 * QR, QR), :], tab[pl.ds(3 * QR, QR), :]
            kv = jnp.dot(xb[span, :], wkv[e], preferred_element_type=F32)
            for b in range(nb):
                keys = turn(kv[b * QR:(b + 1) * QR, :HD], ck, sk).astype(BF16)
                values = kv[b * QR:(b + 1) * QR, HD:].astype(BF16)
                s = dot_t(qout[k0 + b, e], keys)
                w = jnp.where(causal, weights_of(s), 0.0)
                near_t[k0 + b, e] = jnp.broadcast_to(jnp.sum(w, axis=1, keepdims=True), (MSG, HD))
                near_w[k0 + b, e] = jnp.dot(w.astype(BF16), values, preferred_element_type=F32)
            return carry

        lax.fori_loop(0, 2, per_core, 0)
        for b in range(nb):
            for e in range(2):
                q_send(k0 + b, e)
        lax.fori_loop(0, 2, near, 0)

    os_y, os_l = z % 4, z // 4
    os_off = (os_y - y + 4) % 4
    os_group = swap(os_off)
    os_stage = (os_group + 1) // 2
    os_cross = (xl + os_l) % 2
    os_k = os_group * 2 + os_cross

    def o_route(t):
        ox = 2 * (t % 2) + os_l
        hx = (ox + os_cross * (1 + 2 * xh)) % 4
        here = (t // 2 == z) & (hx == x) & (xh == c)
        return here, dev(hx, y, t // 2, xh)

    def o_copy(t, to):
        return remote(oout.at[t], oin.at[os_k, c], so_s.at[t], so_r.at[os_k * 2 + c], to)

    def source():
        for t in range(N):

            @pl.when(jnp.logical_not(o_route(t)[0]))
            def _():
                remote(qin.at[t], qin.at[t], sq_s.at[0], sq_r.at[t], mate).wait_recv()


        def rotate(t, carry):
            r = whose[t]
            q = qin[t].astype(F32)
            qrot[t] = turn(q, turn_c[r][0:1, :], turn_s[r][0:1, :]).astype(BF16)
            return carry

        lax.fori_loop(0, N, rotate, 0)
        col = lax.broadcasted_iota(jnp.int32, (MSG, PAGE), 1)

        def slot(i, state):
            r, p = state
            kv = pool[order[0, i]]
            s = dot_t(qrot[tgt[0, r]], kv[:, :HD])
            w = jnp.where(col < cached_s[r] - PAGE * p, weights_of(s), 0.0)
            more = jnp.full((MSG, HD), p, jnp.int32) > 0
            far_l[i + 1] = w[:, :HD] + w[:, HD:] + jnp.where(more, far_l[i], 0.0)
            pv = jnp.dot(w.astype(BF16), kv[:, HD:], preferred_element_type=F32)
            far_w[i + 1] = pv + jnp.where(more, far_w[i], 0.0)
            last = p + 1 == cnt[0, r]
            return jnp.where(last, jnp.minimum(r + 1, N - 1), r), jnp.where(last, 0, p + 1)

        def two(i, state):
            return slot(2 * i + 1, slot(2 * i, state))

        far_l[0] = jnp.zeros((MSG, HD), F32)
        far_w[0] = jnp.zeros((MSG, HD), F32)
        lax.fori_loop(0, POOL // 2, two, (jnp.int32(0), jnp.int32(0)))
        row = lax.broadcasted_iota(jnp.int32, (16, HD), 0)
        ones = jnp.ones((16, HD), BF16)

        def back(t, carry):
            i = eslot[t]
            sums = far_l[i]
            high = sums.astype(BF16)
            low = (sums - high.astype(F32)).astype(BF16)
            total = dot_t(ones, high) + dot_t(ones, low)
            total_h = total.astype(BF16).astype(F32)
            both = jnp.where(row == 0, total_h, jnp.where(row == 1, total - total_h, 0.0))
            oout[t, pl.ds(0, MSG), :] = far_w[i].astype(BF16)
            oout[t, pl.ds(MSG, 16), :] = both.astype(BF16)
            return carry

        lax.fori_loop(0, N, back, 0)
        for t in range(N):
            here, to = o_route(t)

            @pl.when(here)
            def _():
                own = pltpu.make_async_copy(oout.at[t], oin.at[os_k, c], sl.at[7])
                own.start()
                own.wait()

            @pl.when(jnp.logical_not(here))
            def _():
                o_copy(t, to).start()


    def project(k0, nb):
        for k in range(k0, k0 + nb):
            for e in range(2):

                @pl.when(jnp.logical_not(q_route(k, e)[0]))
                def _():
                    remote(oin.at[k, e], oin.at[k, e], so_s.at[0], so_r.at[k * 2 + e], mate).wait_recv()

        ones = jnp.ones((16, HD), BF16)

        for k in range(k0, k0 + nb):
            for e in range(2):
                far = oin[k, e, pl.ds(0, MSG), :].astype(F32)
                total = lax.dot_general(
                    oin[k, e, pl.ds(MSG, 16), :], ones, (((0,), (0,)), ((), ())), preferred_element_type=F32
                )
                done = ((near_w[k, e] + far) / (near_t[k, e] + total)).astype(BF16)
                att[e, 0, pl.ds(k * QR, QR), :] = done[:QR]
                att[e, 1, pl.ds(k * QR, QR), :] = done[QR:]
        span = pl.ds(k0 * QR, nb * QR)
        mixed = jnp.concatenate([att[e, h, span, :] for e in range(2) for h in range(2)], axis=1)

        def columns(n, carry):
            at = pl.ds(pl.multiple_of(n * COLS, COLS), COLS)
            part[span, at] = jnp.dot(mixed, wo[:, at], preferred_element_type=F32).astype(BF16)
            return carry

        lax.fori_loop(0, STEPS, columns, 0)

    def add(dst, dst_rows, sources):
        def columns(n, carry):
            at = pl.ds(pl.multiple_of(n * COLS, COLS), COLS)
            total = dst[dst_rows, at].astype(F32)
            for ref, its in sources:
                total = total + ref[its, at].astype(F32)
            dst[dst_rows, at] = total.astype(BF16)
            return carry

        lax.fori_loop(0, STEPS, columns, 0)

    def t_copy(i, g, half):
        src = part.at[rows(2 * g + 1, half)]
        return remote(src, rx.at[rows(g, half)], tx_s.at[i], tx_r.at[i], x_back)

    t_copies = [
        t_copy(0, 0, None), t_copy(1, 1, 1), t_copy(2, 2, 0),
        t_copy(3, 3, 0), t_copy(4, 3, 1), t_copy(5, 1, 0), t_copy(6, 2, 1),
    ]
    u_copies = [
        remote(part.at[rows(2, 1)], fin.at[0, pl.ds(HALF, HALF)], ty_s.at[0], ty_r.at[0], y_up),
        remote(part.at[rows(4, 0)], fin.at[1, pl.ds(0, HALF)], ty_s.at[1], ty_r.at[1], y_down),
        remote(part.at[rows(6, 0)], ry.at[pl.ds(0, HALF)], ty_s.at[2], ty_r.at[2], y_up),
        remote(part.at[rows(6, 1)], ry.at[pl.ds(HALF, HALF)], ty_s.at[3], ty_r.at[3], y_down),
        remote(part.at[rows(2, 0)], fin.at[0, pl.ds(0, HALF)], ty_s.at[4], ty_r.at[4], y_up),
        remote(part.at[rows(4, 1)], fin.at[1, pl.ds(HALF, HALF)], ty_s.at[5], ty_r.at[5], y_down),
    ]

    y_copies[0].wait_recv()
    x_copies[1].start()
    y_copies[4].start()
    y_copies[1].wait_recv()
    x_copies[2].start()
    y_copies[5].start()

    for i in range(3):
        local[i].wait()
    w_arrive(0, wq.at[1 - c])
    w_arrive(1, wkv.at[1 - c])
    x_copies[0].wait_recv()
    handle(0, 2)

    y_copies[2].wait_recv()
    x_copies[3].start()
    y_copies[3].wait_recv()
    x_copies[4].start()
    local[4].wait()
    local[5].wait()

    @pl.when(os_stage == 0)
    def _():
        source()

    y_copies[4].wait_recv()
    x_copies[5].start()
    y_copies[5].wait_recv()
    x_copies[6].start()
    for i in range(1, 5):
        x_copies[i].wait_recv()
    handle(2, 4)
    x_copies[5].wait_recv()
    x_copies[6].wait_recv()
    handle(6, 2)

    @pl.when(os_stage != 0)
    def _():
        source()

    w_arrive(2, wo.at[pl.ds(pl.multiple_of((1 - c) * 256, 256), 256)])
    project(0, 2)
    t_copies[0].start()
    project(2, 4)
    t_copies[1].start()
    t_copies[2].start()
    project(6, 2)
    for i in range(3, 7):
        t_copies[i].start()

    t_copies[0].wait_recv()
    t_copies[1].wait_recv()
    add(part, rows(2, 1), [(rx, rows(1, 1))])
    u_copies[0].start()
    t_copies[2].wait_recv()
    add(part, rows(4, 0), [(rx, rows(2, 0))])
    u_copies[1].start()
    t_copies[3].wait_recv()
    add(part, rows(6, 0), [(rx, rows(3, 0))])
    u_copies[2].start()
    t_copies[4].wait_recv()
    add(part, rows(6, 1), [(rx, rows(3, 1))])
    u_copies[3].start()
    t_copies[5].wait_recv()
    u_copies[2].wait_recv()
    add(part, rows(2, 0), [(rx, rows(1, 0)), (ry, pl.ds(0, HALF))])
    u_copies[4].start()
    t_copies[6].wait_recv()
    u_copies[3].wait_recv()
    add(part, rows(4, 1), [(rx, rows(2, 1)), (ry, pl.ds(HALF, HALF))])
    u_copies[5].start()
    u_copies[0].wait_recv()
    u_copies[1].wait_recv()
    u_copies[4].wait_recv()
    u_copies[5].wait_recv()

    def finish(n, carry):
        at = pl.ds(pl.multiple_of(n * COLS, COLS), COLS)
        total = part[pl.ds(0, QR), at].astype(F32) + rx[pl.ds(0, QR), at].astype(F32)
        total = total + fin[0, :, at].astype(F32) + fin[1, :, at].astype(F32)
        out[:, at] = total.astype(BF16)
        return carry

    lax.fori_loop(0, STEPS, finish, 0)

    for copy in y_copies + x_copies + w_copies + t_copies + u_copies:
        copy.wait_send()

    for i in range(N):
        here, to, t = q_route(i // 2, i % 2)

        @pl.when(jnp.logical_not(here))
        def _():
            q_copy(i // 2, i % 2, to, t).wait_send()

        back_here, back_to = o_route(i)

        @pl.when(jnp.logical_not(back_here))
        def _():
            o_copy(i, back_to).wait_send()


def shards(tokens, w_query, w_keyval, w_out, kv_pool, req_target, page_counts, tail_tokens, migrate, pool_order):
    table = jnp.asarray(tables())
    anyspace = pl.BlockSpec(memory_space=pl.ANY)
    smem = pl.BlockSpec(memory_space=pltpu.SMEM)
    dma = pltpu.SemaphoreType.DMA
    return pl.pallas_call(
        kernel,
        out_shape=jax.ShapeDtypeStruct((QR, D), BF16),
        in_specs=[anyspace] * 5 + [smem] * 5 + [anyspace],
        out_specs=pl.BlockSpec(memory_space=pltpu.VMEM),
        scratch_shapes=[
            pltpu.VMEM((8 * QR, D), BF16),
            pltpu.VMEM((2, D, 256), BF16),
            pltpu.VMEM((2, D, 256), BF16),
            pltpu.VMEM((512, D), BF16),
            pltpu.VMEM((POOL, PAGE, 256), BF16),
            pltpu.VMEM((4 * QR + 8, HD), F32),
            pltpu.VMEM((8, 2, MSG, HD), BF16),
            pltpu.VMEM((N, MSG, HD), BF16),
            pltpu.VMEM((N, MSG, HD), BF16),
            pltpu.VMEM((8, 2, MSG, HD), F32),
            pltpu.VMEM((8, 2, MSG, HD), F32),
            pltpu.VMEM((POOL + 1, MSG, HD), F32),
            pltpu.VMEM((POOL + 1, MSG, HD), F32),
            pltpu.VMEM((N, OMSG, HD), BF16),
            pltpu.VMEM((8, 2, OMSG, HD), BF16),
            pltpu.VMEM((2, 2, 8 * QR, HD), BF16),
            pltpu.VMEM((8 * QR, D), BF16),
            pltpu.VMEM((4 * QR, D), BF16),
            pltpu.VMEM((QR, D), BF16),
            pltpu.VMEM((2, QR, D), BF16),
            pltpu.VMEM((N, 8, HD), F32),
            pltpu.VMEM((N, 8, HD), F32),
            pltpu.SMEM((N,), jnp.int32),
            pltpu.SMEM((N,), jnp.int32),
            pltpu.SMEM((N,), jnp.int32),
            dma((8,)),
            dma((3,)), dma((3,)),
            dma((6,)), dma((6,)),
            dma((7,)), dma((7,)),
            dma((N,)), dma((N,)),
            dma((N,)), dma((N,)),
            dma((7,)), dma((7,)),
            dma((6,)), dma((6,)),
        ],
        compiler_params=pltpu.CompilerParams(
            collective_id=0, has_side_effects=True, vmem_limit_bytes=58 * 2**20
        ),
        cost_estimate=pl.CostEstimate(flops=9 * 10**9, bytes_accessed=13 * 10**6, transcendentals=3 * 10**6),
    )(tokens, w_query, w_keyval, w_out, kv_pool, req_target, page_counts, tail_tokens, migrate, pool_order, table)


def solution(mesh):
    return jax.shard_map(
        shards,
        mesh=mesh,
        in_specs=(
            P(("inst", "tp"), None),
            P(None, "tp"),
            P(None, "tp"),
            P("tp", None),
            P("inst", None, "tp"),
            P("inst", None),
            P("inst", None),
            P("inst", None),
            P("inst", None),
            P("inst", None),
        ),
        out_specs=P(("inst", "tp"), None),
        check_vma=False,
    )
```

```python
import math

import jax
import jax.numpy as jnp
import numpy as np
from jax import lax
from jax.experimental import pallas as pl
from jax.experimental.pallas import tpu as pltpu
from jax.sharding import PartitionSpec as P

D = 4608
HEADS = 32
HD = 128
QR = 64
HALF = QR // 2
PAGE = 256
POOL = 32
N = 16
SOFTCAP = 50.0
ROPE_BASE = 10000.0
COLS = 512
STEPS = D // COLS
MSG = 2 * QR
OMSG = MSG + 16
BATCH = 8
MESH = pl.DeviceIdType.MESH
F32 = jnp.float32
BF16 = jnp.bfloat16
SHARP = SOFTCAP * math.log2(math.e)


def tables():
    k = np.arange(HD // 2, dtype=np.float64)
    freq = (ROPE_BASE ** (-2.0 * k / HD)).astype(np.float32)
    angle = np.arange(QR, dtype=np.float64)[:, None] * freq.astype(np.float64)[None, :]
    cos = np.concatenate([np.cos(angle)] * 2, axis=1)
    sin = np.concatenate([-np.sin(angle), np.sin(angle)], axis=1)
    scale = (D // HEADS) ** -0.5 / SOFTCAP
    row = np.tile(np.concatenate([freq, freq])[None, :], (8, 1))
    return np.concatenate([cos * scale, sin * scale, cos, sin, row], axis=0).astype(np.float32)


def swap(i):
    return i + (i // 2) * (1 - 2 * (i % 2))


def turn(v, cos, sin):
    return v * cos + pltpu.roll(v, HD // 2, 1) * sin


def weights_of(scores):
    return jnp.exp2(SHARP * jnp.tanh(scores))


def dot_t(a, b):
    return lax.dot_general(a, b, (((1,), (1,)), ((), ())), preferred_element_type=F32)


def kernel(
    tok, wq_in, wkv_in, wo_in, pool_in, tgt, cnt, tail, mig, order, tab_in,
    out,
    xb, wq, wkv, wo, pool, tab, qout, qin, qrot, near_w, near_t, far_w, far_l, oout, oin, att,
    part, rx, ry, fin, turn_c, turn_s,
    cached_s, eslot, whose,
    sl, sw_s, sw_r, sy_s, sy_r, sx_s, sx_r, sq_s, sq_r, so_s, so_r, tx_s, tx_r, ty_s, ty_r,
):
    inst = lax.axis_index("inst")
    j = lax.axis_index("tp")
    z = inst // 2
    xh = inst % 2
    xl = j // 8
    y = (j // 2) % 4
    c = j % 2
    x = 2 * xh + xl

    def dev(px, py, pz, pc):
        return (pz * 2 + px // 2, (px % 2) * 8 + py * 2 + pc)

    up, down = (y + 1) % 4, (y + 3) % 4
    fx = (x + 1 + 2 * c) % 4
    bx = (x + 3 + 2 * c) % 4
    y_up, y_down = dev(x, up, z, c), dev(x, down, z, c)
    x_fwd, x_back = dev(fx, y, z, c), dev(bx, y, z, c)
    mate = dev(x, y, z, 1 - c)

    def remote(src, dst, ss, rs, to):
        return pltpu.make_async_remote_copy(
            src_ref=src, dst_ref=dst, send_sem=ss, recv_sem=rs, device_id=to, device_id_type=MESH
        )

    local = [
        pltpu.make_async_copy(tok, xb.at[pl.ds(0, QR)], sl.at[0]),
        pltpu.make_async_copy(wq_in, wq.at[c], sl.at[1]),
        pltpu.make_async_copy(wkv_in, wkv.at[c], sl.at[2]),
        pltpu.make_async_copy(tab_in, tab, sl.at[3]),
        pltpu.make_async_copy(wo_in, wo.at[pl.ds(pl.multiple_of(c * 256, 256), 256)], sl.at[4]),
        pltpu.make_async_copy(pool_in, pool, sl.at[5]),
    ]
    for copy in local:
        copy.start()

    barrier = pltpu.get_barrier_semaphore()
    for to in (y_up, y_down, x_fwd, x_back):
        pl.semaphore_signal(barrier, inc=1, device_id=to, device_id_type=MESH)

    def greet(i, carry):
        to = ((i // 4) * 2 + (i // 2) % 2, xl * 8 + y * 2 + i % 2)

        @pl.when((to[0] != inst) | (to[1] != j))
        def _():
            pl.semaphore_signal(barrier, inc=1, device_id=to, device_id_type=MESH)

        return carry

    lax.fori_loop(0, 32, greet, 0)
    pl.semaphore_wait(barrier, 35)

    def rows(k, half=None):
        if half is None:
            return pl.ds(k * QR, QR)
        return pl.ds(k * QR + half * HALF, HALF)

    def tok_half(half):
        return tok.at[pl.ds(half * HALF, HALF)]

    y_copies = [
        remote(tok_half(0), xb.at[rows(4, 0)], sy_s.at[0], sy_r.at[0], y_up),
        remote(tok_half(1), xb.at[rows(2, 1)], sy_s.at[1], sy_r.at[1], y_down),
        remote(tok_half(1), xb.at[rows(4, 1)], sy_s.at[2], sy_r.at[2], y_up),
        remote(tok_half(0), xb.at[rows(2, 0)], sy_s.at[3], sy_r.at[3], y_down),
        remote(xb.at[rows(4, 0)], xb.at[rows(6, 0)], sy_s.at[4], sy_r.at[4], y_up),
        remote(xb.at[rows(2, 1)], xb.at[rows(6, 1)], sy_s.at[5], sy_r.at[5], y_down),
    ]

    def x_copy(i, k, half):
        return remote(xb.at[rows(k, half)], xb.at[rows(k + 1, half)], sx_s.at[i], sx_r.at[i], x_fwd)

    x_copies = [
        remote(tok, xb.at[rows(1)], sx_s.at[0], sx_r.at[0], x_fwd),
        x_copy(1, 4, 0), x_copy(2, 2, 1), x_copy(3, 4, 1), x_copy(4, 2, 0), x_copy(5, 6, 0), x_copy(6, 6, 1),
    ]
    w_copies = [
        remote(wq_in, wq.at[c], sw_s.at[0], sw_r.at[0], mate),
        remote(wkv_in, wkv.at[c], sw_s.at[1], sw_r.at[1], mate),
        remote(wo_in, wo.at[pl.ds(pl.multiple_of(c * 256, 256), 256)], sw_s.at[2], sw_r.at[2], mate),
    ]

    def w_arrive(i, ref):
        pltpu.make_async_copy(ref, ref, sw_r.at[i]).wait()

    y_copies[0].start()
    y_copies[1].start()
    x_copies[0].start()
    y_copies[2].start()
    y_copies[3].start()
    w_copies[0].start()
    w_copies[1].start()
    w_copies[2].start()

    local[3].wait()
    freq = tab[pl.ds(4 * QR, 8), :]
    sign = jnp.where(lax.broadcasted_iota(jnp.int32, (8, HD), 1) < HD // 2, -1.0, 1.0)

    def request(r, end):
        cached = mig[0, r] * ((cnt[0, r] - 1) * PAGE + tail[0, r])
        cached_s[r] = cached
        angle = cached.astype(F32) * freq
        turn_c[r] = jnp.cos(angle)
        turn_s[r] = jnp.sin(angle) * sign
        return end

    lax.fori_loop(0, N, request, 0)

    def ends(t, carry):
        def one(r, state):
            end, found, who = state
            end = end + cnt[0, r]
            hit = tgt[0, r] == t
            return end, jnp.where(hit, end, found), jnp.where(hit, r, who)

        state = lax.fori_loop(0, N, one, (jnp.int32(0), jnp.int32(0), jnp.int32(0)))
        eslot[t] = state[1]
        whose[t] = state[2]
        return carry

    lax.fori_loop(0, N, ends, 0)

    def q_route(k, e):
        group, cross = k // 2, k % 2
        offset = swap(group)
        ox = x + cross * (bx - x)
        oy = (y + offset) % 4
        zs = (ox % 2) * 4 + oy
        here = (zs == z) & (xh == c) & (e == c)
        return here, dev(2 * c + xl, y, zs, e), z * 2 + ox // 2

    def q_copy(k, e, to, t):
        return remote(qout.at[k, e], qin.at[t], sq_s.at[k * 2 + e], sq_r.at[t], to)

    def q_send(k, e):
        here, to, t = q_route(k, e)

        @pl.when(here)
        def _():
            own = pltpu.make_async_copy(qout.at[k, e], qin.at[t], sl.at[6])
            own.start()
            own.wait()

        @pl.when(jnp.logical_not(here))
        def _():
            q_copy(k, e, to, t).start()

    causal = (
        lax.broadcasted_iota(jnp.int32, (MSG, QR), 0) % QR
        >= lax.broadcasted_iota(jnp.int32, (MSG, QR), 1)
    )

    def handle(k0, nb):
        span = pl.ds(k0 * QR, nb * QR)

        def per_core(e, carry):
            cq, sq = tab[pl.ds(0, QR), :], tab[pl.ds(QR, QR), :]
            q = jnp.dot(xb[span, :], wq[e], preferred_element_type=F32)
            for b in range(nb):
                for h in range(2):
                    v = q[b * QR:(b + 1) * QR, h * HD:(h + 1) * HD]
                    qout[k0 + b, e, pl.ds(h * QR, QR), :] = turn(v, cq, sq).astype(BF16)
            return carry

        def near(e, carry):
            ck, sk = tab[pl.ds(2 * QR, QR), :], tab[pl.ds(3 * QR, QR), :]
            kv = jnp.dot(xb[span, :], wkv[e], preferred_element_type=F32)
            for b in range(nb):
                keys = turn(kv[b * QR:(b + 1) * QR, :HD], ck, sk).astype(BF16)
                values = kv[b * QR:(b + 1) * QR, HD:].astype(BF16)
                s = dot_t(qout[k0 + b, e], keys)
                w = jnp.where(causal, weights_of(s), 0.0)
                near_t[k0 + b, e] = jnp.broadcast_to(jnp.sum(w, axis=1, keepdims=True), (MSG, HD))
                near_w[k0 + b, e] = jnp.dot(w.astype(BF16), values, preferred_element_type=F32)
            return carry

        lax.fori_loop(0, 2, per_core, 0)
        for b in range(nb):
            for e in range(2):
                q_send(k0 + b, e)
        lax.fori_loop(0, 2, near, 0)

    os_y, os_l = z % 4, z // 4
    os_off = (os_y - y + 4) % 4
    os_group = swap(os_off)
    os_stage = (os_group + 1) // 2
    os_cross = (xl + os_l) % 2
    os_k = os_group * 2 + os_cross

    def o_route(t):
        ox = 2 * (t % 2) + os_l
        hx = (ox + os_cross * (1 + 2 * xh)) % 4
        here = (t // 2 == z) & (hx == x) & (xh == c)
        return here, dev(hx, y, t // 2, xh)

    def o_copy(t, to):
        return remote(oout.at[t], oin.at[os_k, c], so_s.at[t], so_r.at[os_k * 2 + c], to)

    def source():
        for t in range(N):

            @pl.when(jnp.logical_not(o_route(t)[0]))
            def _():
                remote(qin.at[t], qin.at[t], sq_s.at[0], sq_r.at[t], mate).wait_recv()


        def rotate(t, carry):
            r = whose[t]
            q = qin[t].astype(F32)
            qrot[t] = turn(q, turn_c[r][0:1, :], turn_s[r][0:1, :]).astype(BF16)
            return carry

        lax.fori_loop(0, N, rotate, 0, unroll=4)
        col = lax.broadcasted_iota(jnp.int32, (MSG, PAGE), 1)

        def slots(i, state):
            r, p = state
            owner, page = [], []
            for u in range(BATCH):
                owner.append(r)
                page.append(p)
                last = p + 1 == cnt[0, r]
                r, p = jnp.where(last, jnp.minimum(r + 1, N - 1), r), jnp.where(last, 0, p + 1)
            kv = [pool[order[0, BATCH * i + u]] for u in range(BATCH)]
            s = [dot_t(qrot[tgt[0, owner[u]]], kv[u][:, :HD]) for u in range(BATCH)]
            w = [
                jnp.where(col < cached_s[owner[u]] - PAGE * page[u], weights_of(s[u]), 0.0)
                for u in range(BATCH)
            ]
            pv = [
                jnp.dot(w[u].astype(BF16), kv[u][:, HD:], preferred_element_type=F32) for u in range(BATCH)
            ]
            sum_l, sum_w = far_l[BATCH * i], far_w[BATCH * i]
            for u in range(BATCH):
                more = jnp.full((MSG, HD), page[u], jnp.int32) > 0
                sum_l = w[u][:, :HD] + w[u][:, HD:] + jnp.where(more, sum_l, 0.0)
                sum_w = pv[u] + jnp.where(more, sum_w, 0.0)
                far_l[BATCH * i + u + 1] = sum_l
                far_w[BATCH * i + u + 1] = sum_w
            return r, p

        far_l[0] = jnp.zeros((MSG, HD), F32)
        far_w[0] = jnp.zeros((MSG, HD), F32)
        lax.fori_loop(0, POOL // BATCH, slots, (jnp.int32(0), jnp.int32(0)))
        row = lax.broadcasted_iota(jnp.int32, (16, HD), 0)
        ones = jnp.ones((16, HD), BF16)

        def back(t, carry):
            i = eslot[t]
            sums = far_l[i]
            high = sums.astype(BF16)
            low = (sums - high.astype(F32)).astype(BF16)
            total = dot_t(ones, high) + dot_t(ones, low)
            total_h = total.astype(BF16).astype(F32)
            both = jnp.where(row == 0, total_h, jnp.where(row == 1, total - total_h, 0.0))
            oout[t, pl.ds(0, MSG), :] = far_w[i].astype(BF16)
            oout[t, pl.ds(MSG, 16), :] = both.astype(BF16)
            return carry

        lax.fori_loop(0, N, back, 0, unroll=4)
        for t in range(N):
            here, to = o_route(t)

            @pl.when(here)
            def _():
                own = pltpu.make_async_copy(oout.at[t], oin.at[os_k, c], sl.at[7])
                own.start()
                own.wait()

            @pl.when(jnp.logical_not(here))
            def _():
                o_copy(t, to).start()


    def project(k0, nb):
        for k in range(k0, k0 + nb):
            for e in range(2):

                @pl.when(jnp.logical_not(q_route(k, e)[0]))
                def _():
                    remote(oin.at[k, e], oin.at[k, e], so_s.at[0], so_r.at[k * 2 + e], mate).wait_recv()

        ones = jnp.ones((16, HD), BF16)

        for k in range(k0, k0 + nb):
            for e in range(2):
                far = oin[k, e, pl.ds(0, MSG), :].astype(F32)
                total = lax.dot_general(
                    oin[k, e, pl.ds(MSG, 16), :], ones, (((0,), (0,)), ((), ())), preferred_element_type=F32
                )
                done = ((near_w[k, e] + far) / (near_t[k, e] + total)).astype(BF16)
                att[e, 0, pl.ds(k * QR, QR), :] = done[:QR]
                att[e, 1, pl.ds(k * QR, QR), :] = done[QR:]
        span = pl.ds(k0 * QR, nb * QR)
        mixed = jnp.concatenate([att[e, h, span, :] for e in range(2) for h in range(2)], axis=1)

        def columns(n, carry):
            at = pl.ds(pl.multiple_of(n * COLS, COLS), COLS)
            part[span, at] = jnp.dot(mixed, wo[:, at], preferred_element_type=F32).astype(BF16)
            return carry

        lax.fori_loop(0, STEPS, columns, 0)

    def add(dst, dst_rows, sources):
        def columns(n, carry):
            at = pl.ds(pl.multiple_of(n * COLS, COLS), COLS)
            total = dst[dst_rows, at].astype(F32)
            for ref, its in sources:
                total = total + ref[its, at].astype(F32)
            dst[dst_rows, at] = total.astype(BF16)
            return carry

        lax.fori_loop(0, STEPS, columns, 0)

    def t_copy(i, g, half):
        src = part.at[rows(2 * g + 1, half)]
        return remote(src, rx.at[rows(g, half)], tx_s.at[i], tx_r.at[i], x_back)

    t_copies = [
        t_copy(0, 0, None), t_copy(1, 1, 1), t_copy(2, 2, 0),
        t_copy(3, 3, 0), t_copy(4, 3, 1), t_copy(5, 1, 0), t_copy(6, 2, 1),
    ]
    u_copies = [
        remote(part.at[rows(2, 1)], fin.at[0, pl.ds(HALF, HALF)], ty_s.at[0], ty_r.at[0], y_up),
        remote(part.at[rows(4, 0)], fin.at[1, pl.ds(0, HALF)], ty_s.at[1], ty_r.at[1], y_down),
        remote(part.at[rows(6, 0)], ry.at[pl.ds(0, HALF)], ty_s.at[2], ty_r.at[2], y_up),
        remote(part.at[rows(6, 1)], ry.at[pl.ds(HALF, HALF)], ty_s.at[3], ty_r.at[3], y_down),
        remote(part.at[rows(2, 0)], fin.at[0, pl.ds(0, HALF)], ty_s.at[4], ty_r.at[4], y_up),
        remote(part.at[rows(4, 1)], fin.at[1, pl.ds(HALF, HALF)], ty_s.at[5], ty_r.at[5], y_down),
    ]

    y_copies[0].wait_recv()
    x_copies[1].start()
    y_copies[4].start()
    y_copies[1].wait_recv()
    x_copies[2].start()
    y_copies[5].start()

    for i in range(3):
        local[i].wait()
    w_arrive(0, wq.at[1 - c])
    w_arrive(1, wkv.at[1 - c])
    x_copies[0].wait_recv()
    handle(0, 2)

    y_copies[2].wait_recv()
    x_copies[3].start()
    y_copies[3].wait_recv()
    x_copies[4].start()
    local[4].wait()
    local[5].wait()

    @pl.when(os_stage == 0)
    def _():
        source()

    y_copies[4].wait_recv()
    x_copies[5].start()
    y_copies[5].wait_recv()
    x_copies[6].start()
    for i in range(1, 5):
        x_copies[i].wait_recv()
    handle(2, 4)
    x_copies[5].wait_recv()
    x_copies[6].wait_recv()
    handle(6, 2)

    @pl.when(os_stage != 0)
    def _():
        source()

    w_arrive(2, wo.at[pl.ds(pl.multiple_of((1 - c) * 256, 256), 256)])
    project(0, 2)
    t_copies[0].start()
    project(2, 4)
    t_copies[1].start()
    t_copies[2].start()
    project(6, 2)
    for i in range(3, 7):
        t_copies[i].start()

    t_copies[0].wait_recv()
    t_copies[1].wait_recv()
    add(part, rows(2, 1), [(rx, rows(1, 1))])
    u_copies[0].start()
    t_copies[2].wait_recv()
    add(part, rows(4, 0), [(rx, rows(2, 0))])
    u_copies[1].start()
    t_copies[3].wait_recv()
    add(part, rows(6, 0), [(rx, rows(3, 0))])
    u_copies[2].start()
    t_copies[4].wait_recv()
    add(part, rows(6, 1), [(rx, rows(3, 1))])
    u_copies[3].start()
    t_copies[5].wait_recv()
    u_copies[2].wait_recv()
    add(part, rows(2, 0), [(rx, rows(1, 0)), (ry, pl.ds(0, HALF))])
    u_copies[4].start()
    t_copies[6].wait_recv()
    u_copies[3].wait_recv()
    add(part, rows(4, 1), [(rx, rows(2, 1)), (ry, pl.ds(HALF, HALF))])
    u_copies[5].start()
    u_copies[0].wait_recv()
    u_copies[1].wait_recv()
    u_copies[4].wait_recv()
    u_copies[5].wait_recv()

    def finish(n, carry):
        at = pl.ds(pl.multiple_of(n * COLS, COLS), COLS)
        total = part[pl.ds(0, QR), at].astype(F32) + rx[pl.ds(0, QR), at].astype(F32)
        total = total + fin[0, :, at].astype(F32) + fin[1, :, at].astype(F32)
        out[:, at] = total.astype(BF16)
        return carry

    lax.fori_loop(0, STEPS, finish, 0)

    for copy in y_copies + x_copies + w_copies + t_copies + u_copies:
        copy.wait_send()

    for i in range(N):
        here, to, t = q_route(i // 2, i % 2)

        @pl.when(jnp.logical_not(here))
        def _():
            q_copy(i // 2, i % 2, to, t).wait_send()

        back_here, back_to = o_route(i)

        @pl.when(jnp.logical_not(back_here))
        def _():
            o_copy(i, back_to).wait_send()


def shards(tokens, w_query, w_keyval, w_out, kv_pool, req_target, page_counts, tail_tokens, migrate, pool_order):
    table = jnp.asarray(tables())
    anyspace = pl.BlockSpec(memory_space=pl.ANY)
    smem = pl.BlockSpec(memory_space=pltpu.SMEM)
    dma = pltpu.SemaphoreType.DMA
    return pl.pallas_call(
        kernel,
        out_shape=jax.ShapeDtypeStruct((QR, D), BF16),
        in_specs=[anyspace] * 5 + [smem] * 5 + [anyspace],
        out_specs=pl.BlockSpec(memory_space=pltpu.VMEM),
        scratch_shapes=[
            pltpu.VMEM((8 * QR, D), BF16),
            pltpu.VMEM((2, D, 256), BF16),
            pltpu.VMEM((2, D, 256), BF16),
            pltpu.VMEM((512, D), BF16),
            pltpu.VMEM((POOL, PAGE, 256), BF16),
            pltpu.VMEM((4 * QR + 8, HD), F32),
            pltpu.VMEM((8, 2, MSG, HD), BF16),
            pltpu.VMEM((N, MSG, HD), BF16),
            pltpu.VMEM((N, MSG, HD), BF16),
            pltpu.VMEM((8, 2, MSG, HD), F32),
            pltpu.VMEM((8, 2, MSG, HD), F32),
            pltpu.VMEM((POOL + 1, MSG, HD), F32),
            pltpu.VMEM((POOL + 1, MSG, HD), F32),
            pltpu.VMEM((N, OMSG, HD), BF16),
            pltpu.VMEM((8, 2, OMSG, HD), BF16),
            pltpu.VMEM((2, 2, 8 * QR, HD), BF16),
            pltpu.VMEM((8 * QR, D), BF16),
            pltpu.VMEM((4 * QR, D), BF16),
            pltpu.VMEM((QR, D), BF16),
            pltpu.VMEM((2, QR, D), BF16),
            pltpu.VMEM((N, 8, HD), F32),
            pltpu.VMEM((N, 8, HD), F32),
            pltpu.SMEM((N,), jnp.int32),
            pltpu.SMEM((N,), jnp.int32),
            pltpu.SMEM((N,), jnp.int32),
            dma((8,)),
            dma((3,)), dma((3,)),
            dma((6,)), dma((6,)),
            dma((7,)), dma((7,)),
            dma((N,)), dma((N,)),
            dma((N,)), dma((N,)),
            dma((7,)), dma((7,)),
            dma((6,)), dma((6,)),
        ],
        compiler_params=pltpu.CompilerParams(
            collective_id=0, has_side_effects=True, vmem_limit_bytes=58 * 2**20
        ),
        cost_estimate=pl.CostEstimate(flops=9 * 10**9, bytes_accessed=13 * 10**6, transcendentals=3 * 10**6),
    )(tokens, w_query, w_keyval, w_out, kv_pool, req_target, page_counts, tail_tokens, migrate, pool_order, table)


def solution(mesh):
    return jax.shard_map(
        shards,
        mesh=mesh,
        in_specs=(
            P(("inst", "tp"), None),
            P(None, "tp"),
            P(None, "tp"),
            P("tp", None),
            P("inst", None, "tp"),
            P("inst", None),
            P("inst", None),
            P("inst", None),
            P("inst", None),
            P("inst", None),
        ),
        out_specs=P(("inst", "tp"), None),
        check_vma=False,
    )
```

```python
import math

import jax
import jax.numpy as jnp
import numpy as np
from jax import lax
from jax.experimental import pallas as pl
from jax.experimental.pallas import tpu as pltpu
from jax.sharding import PartitionSpec as P

D = 4608
HEADS = 32
HD = 128
QR = 64
HALF = QR // 2
PAGE = 256
POOL = 32
N = 16
SOFTCAP = 50.0
ROPE_BASE = 10000.0
COLS = 512
STEPS = D // COLS
MSG = 2 * QR
OMSG = MSG + 16
BATCH = 8
MESH = pl.DeviceIdType.MESH
F32 = jnp.float32
BF16 = jnp.bfloat16
SHARP = SOFTCAP * math.log2(math.e)


def tables():
    k = np.arange(HD // 2, dtype=np.float64)
    freq = (ROPE_BASE ** (-2.0 * k / HD)).astype(np.float32)
    angle = np.arange(QR, dtype=np.float64)[:, None] * freq.astype(np.float64)[None, :]
    cos = np.concatenate([np.cos(angle)] * 2, axis=1)
    sin = np.concatenate([-np.sin(angle), np.sin(angle)], axis=1)
    scale = (D // HEADS) ** -0.5 / SOFTCAP
    row = np.tile(np.concatenate([freq, freq])[None, :], (8, 1))
    return np.concatenate([cos * scale, sin * scale, cos, sin, row], axis=0).astype(np.float32)


def swap(i):
    return i + (i // 2) * (1 - 2 * (i % 2))


def turn(v, cos, sin):
    return v * cos + pltpu.roll(v, HD // 2, 1) * sin


def weights_of(scores):
    return jnp.exp2(SHARP * jnp.tanh(scores))


def dot_t(a, b):
    return lax.dot_general(a, b, (((1,), (1,)), ((), ())), preferred_element_type=F32)


def kernel(
    tok, wq_in, wkv_in, wo_in, pool_in, tgt, cnt, tail, mig, order, tab_in,
    out,
    xb, wq, wkv, wo, pool, tab, qout, qin, qrot, near_w, near_t, far_w, far_l, oout, oin, att,
    part, rx, ry, fin, turn_c, turn_s,
    cached_s, eslot, whose,
    sl, sw_s, sw_r, sy_s, sy_r, sx_s, sx_r, sq_s, sq_r, so_s, so_r, tx_s, tx_r, ty_s, ty_r,
):
    inst = lax.axis_index("inst")
    j = lax.axis_index("tp")
    z = inst // 2
    xh = inst % 2
    xl = j // 8
    y = (j // 2) % 4
    c = j % 2
    x = 2 * xh + xl

    def dev(px, py, pz, pc):
        return (pz * 2 + px // 2, (px % 2) * 8 + py * 2 + pc)

    up, down = (y + 1) % 4, (y + 3) % 4
    fx = (x + 1 + 2 * c) % 4
    bx = (x + 3 + 2 * c) % 4
    y_up, y_down = dev(x, up, z, c), dev(x, down, z, c)
    x_fwd, x_back = dev(fx, y, z, c), dev(bx, y, z, c)
    mate = dev(x, y, z, 1 - c)

    def remote(src, dst, ss, rs, to):
        return pltpu.make_async_remote_copy(
            src_ref=src, dst_ref=dst, send_sem=ss, recv_sem=rs, device_id=to, device_id_type=MESH
        )

    local = [
        pltpu.make_async_copy(tok, xb.at[pl.ds(0, QR)], sl.at[0]),
        pltpu.make_async_copy(wq_in, wq.at[c], sl.at[1]),
        pltpu.make_async_copy(wkv_in, wkv.at[c], sl.at[2]),
        pltpu.make_async_copy(tab_in, tab, sl.at[3]),
        pltpu.make_async_copy(wo_in, wo.at[pl.ds(pl.multiple_of(c * 256, 256), 256)], sl.at[4]),
        pltpu.make_async_copy(pool_in, pool, sl.at[5]),
    ]
    for copy in local:
        copy.start()

    barrier = pltpu.get_barrier_semaphore()
    for to in (y_up, y_down, x_fwd, x_back):
        pl.semaphore_signal(barrier, inc=1, device_id=to, device_id_type=MESH)

    def greet(i, carry):
        to = ((i // 4) * 2 + (i // 2) % 2, xl * 8 + y * 2 + i % 2)

        @pl.when((to[0] != inst) | (to[1] != j))
        def _():
            pl.semaphore_signal(barrier, inc=1, device_id=to, device_id_type=MESH)

        return carry

    lax.fori_loop(0, 32, greet, 0)
    pl.semaphore_wait(barrier, 35)

    def rows(k, half=None):
        if half is None:
            return pl.ds(k * QR, QR)
        return pl.ds(k * QR + half * HALF, HALF)

    def tok_half(half):
        return tok.at[pl.ds(half * HALF, HALF)]

    y_copies = [
        remote(tok_half(0), xb.at[rows(2, 0)], sy_s.at[0], sy_r.at[0], y_up),
        remote(tok_half(1), xb.at[rows(1, 1)], sy_s.at[1], sy_r.at[1], y_down),
        remote(tok_half(1), xb.at[rows(2, 1)], sy_s.at[2], sy_r.at[2], y_up),
        remote(tok_half(0), xb.at[rows(1, 0)], sy_s.at[3], sy_r.at[3], y_down),
        remote(xb.at[rows(2, 0)], xb.at[rows(3, 0)], sy_s.at[4], sy_r.at[4], y_up),
        remote(xb.at[rows(1, 1)], xb.at[rows(3, 1)], sy_s.at[5], sy_r.at[5], y_down),
    ]

    def x_copy(i, k, half):
        return remote(xb.at[rows(k, half)], xb.at[rows(k + 4, half)], sx_s.at[i], sx_r.at[i], x_fwd)

    x_copies = [
        remote(tok, xb.at[rows(4)], sx_s.at[0], sx_r.at[0], x_fwd),
        x_copy(1, 2, 0), x_copy(2, 1, 1), x_copy(3, 2, 1), x_copy(4, 1, 0), x_copy(5, 3, 0), x_copy(6, 3, 1),
    ]
    w_copies = [
        remote(wq_in, wq.at[c], sw_s.at[0], sw_r.at[0], mate),
        remote(wkv_in, wkv.at[c], sw_s.at[1], sw_r.at[1], mate),
        remote(wo_in, wo.at[pl.ds(pl.multiple_of(c * 256, 256), 256)], sw_s.at[2], sw_r.at[2], mate),
    ]

    def w_arrive(i, ref):
        pltpu.make_async_copy(ref, ref, sw_r.at[i]).wait()

    y_copies[0].start()
    y_copies[1].start()
    x_copies[0].start()
    y_copies[2].start()
    y_copies[3].start()
    w_copies[0].start()
    w_copies[1].start()
    w_copies[2].start()

    local[3].wait()
    freq = tab[pl.ds(4 * QR, 8), :]
    sign = jnp.where(lax.broadcasted_iota(jnp.int32, (8, HD), 1) < HD // 2, -1.0, 1.0)

    def request(r, end):
        cached = mig[0, r] * ((cnt[0, r] - 1) * PAGE + tail[0, r])
        cached_s[r] = cached
        angle = cached.astype(F32) * freq
        turn_c[r] = jnp.cos(angle)
        turn_s[r] = jnp.sin(angle) * sign
        return end

    lax.fori_loop(0, N, request, 0)

    def ends(t, carry):
        def one(r, state):
            end, found, who = state
            end = end + cnt[0, r]
            hit = tgt[0, r] == t
            return end, jnp.where(hit, end, found), jnp.where(hit, r, who)

        state = lax.fori_loop(0, N, one, (jnp.int32(0), jnp.int32(0), jnp.int32(0)))
        eslot[t] = state[1]
        whose[t] = state[2]
        return carry

    lax.fori_loop(0, N, ends, 0)

    def q_route(k, e):
        group, cross = k % 4, k // 4
        offset = swap(group)
        ox = x + cross * (bx - x)
        oy = (y + offset) % 4
        zs = (ox % 2) * 4 + oy
        here = (zs == z) & (xh == c) & (e == c)
        return here, dev(2 * c + xl, y, zs, e), z * 2 + ox // 2

    def q_copy(k, e, to, t):
        return remote(qout.at[k, e], qin.at[t], sq_s.at[k * 2 + e], sq_r.at[t], to)

    def q_send(k, e):
        here, to, t = q_route(k, e)

        @pl.when(here)
        def _():
            own = pltpu.make_async_copy(qout.at[k, e], qin.at[t], sl.at[6])
            own.start()
            own.wait()

        @pl.when(jnp.logical_not(here))
        def _():
            q_copy(k, e, to, t).start()

    causal = (
        lax.broadcasted_iota(jnp.int32, (MSG, QR), 0) % QR
        >= lax.broadcasted_iota(jnp.int32, (MSG, QR), 1)
    )

    def handle(k0, nb):
        span = pl.ds(k0 * QR, nb * QR)

        def per_core(e, carry):
            cq, sq = tab[pl.ds(0, QR), :], tab[pl.ds(QR, QR), :]
            q = jnp.dot(xb[span, :], wq[e], preferred_element_type=F32)
            for b in range(nb):
                for h in range(2):
                    v = q[b * QR:(b + 1) * QR, h * HD:(h + 1) * HD]
                    qout[k0 + b, e, pl.ds(h * QR, QR), :] = turn(v, cq, sq).astype(BF16)
            return carry

        def near(e, carry):
            ck, sk = tab[pl.ds(2 * QR, QR), :], tab[pl.ds(3 * QR, QR), :]
            kv = jnp.dot(xb[span, :], wkv[e], preferred_element_type=F32)
            for b in range(nb):
                keys = turn(kv[b * QR:(b + 1) * QR, :HD], ck, sk).astype(BF16)
                values = kv[b * QR:(b + 1) * QR, HD:].astype(BF16)
                s = dot_t(qout[k0 + b, e], keys)
                w = jnp.where(causal, weights_of(s), 0.0)
                near_t[k0 + b, e] = jnp.broadcast_to(jnp.sum(w, axis=1, keepdims=True), (MSG, HD))
                near_w[k0 + b, e] = jnp.dot(w.astype(BF16), values, preferred_element_type=F32)
            return carry

        lax.fori_loop(0, 2, per_core, 0)
        for b in range(nb):
            for e in range(2):
                q_send(k0 + b, e)
        lax.fori_loop(0, 2, near, 0)

    os_y, os_l = z % 4, z // 4
    os_off = (os_y - y + 4) % 4
    os_group = swap(os_off)
    os_stage = (os_group + 1) // 2
    os_cross = (xl + os_l) % 2
    os_k = os_group + 4 * os_cross

    def o_route(t):
        ox = 2 * (t % 2) + os_l
        hx = (ox + os_cross * (1 + 2 * xh)) % 4
        here = (t // 2 == z) & (hx == x) & (xh == c)
        return here, dev(hx, y, t // 2, xh)

    def o_copy(t, to):
        return remote(oout.at[t], oin.at[os_k, c], so_s.at[t], so_r.at[os_k * 2 + c], to)

    def source():
        for t in range(N):

            @pl.when(jnp.logical_not(o_route(t)[0]))
            def _():
                remote(qin.at[t], qin.at[t], sq_s.at[0], sq_r.at[t], mate).wait_recv()


        def rotate(t, carry):
            r = whose[t]
            q = qin[t].astype(F32)
            qrot[t] = turn(q, turn_c[r][0:1, :], turn_s[r][0:1, :]).astype(BF16)
            return carry

        lax.fori_loop(0, N, rotate, 0, unroll=4)
        col = lax.broadcasted_iota(jnp.int32, (MSG, PAGE), 1)

        def slots(i, state):
            r, p = state
            owner, page = [], []
            for u in range(BATCH):
                owner.append(r)
                page.append(p)
                last = p + 1 == cnt[0, r]
                r, p = jnp.where(last, jnp.minimum(r + 1, N - 1), r), jnp.where(last, 0, p + 1)
            kv = [pool[order[0, BATCH * i + u]] for u in range(BATCH)]
            s = [dot_t(qrot[tgt[0, owner[u]]], kv[u][:, :HD]) for u in range(BATCH)]
            w = [
                jnp.where(col < cached_s[owner[u]] - PAGE * page[u], weights_of(s[u]), 0.0)
                for u in range(BATCH)
            ]
            pv = [
                jnp.dot(w[u].astype(BF16), kv[u][:, HD:], preferred_element_type=F32) for u in range(BATCH)
            ]
            sum_l, sum_w = far_l[BATCH * i], far_w[BATCH * i]
            for u in range(BATCH):
                more = jnp.full((MSG, HD), page[u], jnp.int32) > 0
                sum_l = w[u][:, :HD] + w[u][:, HD:] + jnp.where(more, sum_l, 0.0)
                sum_w = pv[u] + jnp.where(more, sum_w, 0.0)
                far_l[BATCH * i + u + 1] = sum_l
                far_w[BATCH * i + u + 1] = sum_w
            return r, p

        far_l[0] = jnp.zeros((MSG, HD), F32)
        far_w[0] = jnp.zeros((MSG, HD), F32)
        lax.fori_loop(0, POOL // BATCH, slots, (jnp.int32(0), jnp.int32(0)))
        row = lax.broadcasted_iota(jnp.int32, (16, HD), 0)
        ones = jnp.ones((16, HD), BF16)

        def back(t, carry):
            i = eslot[t]
            sums = far_l[i]
            high = sums.astype(BF16)
            low = (sums - high.astype(F32)).astype(BF16)
            total = dot_t(ones, high) + dot_t(ones, low)
            total_h = total.astype(BF16).astype(F32)
            both = jnp.where(row == 0, total_h, jnp.where(row == 1, total - total_h, 0.0))
            oout[t, pl.ds(0, MSG), :] = far_w[i].astype(BF16)
            oout[t, pl.ds(MSG, 16), :] = both.astype(BF16)
            return carry

        lax.fori_loop(0, N, back, 0, unroll=4)
        for t in range(N):
            here, to = o_route(t)

            @pl.when(here)
            def _():
                own = pltpu.make_async_copy(oout.at[t], oin.at[os_k, c], sl.at[7])
                own.start()
                own.wait()

            @pl.when(jnp.logical_not(here))
            def _():
                o_copy(t, to).start()


    def project(k0, nb):
        for k in range(k0, k0 + nb):
            for e in range(2):

                @pl.when(jnp.logical_not(q_route(k, e)[0]))
                def _():
                    remote(oin.at[k, e], oin.at[k, e], so_s.at[0], so_r.at[k * 2 + e], mate).wait_recv()

        ones = jnp.ones((16, HD), BF16)

        for k in range(k0, k0 + nb):
            for e in range(2):
                far = oin[k, e, pl.ds(0, MSG), :].astype(F32)
                total = lax.dot_general(
                    oin[k, e, pl.ds(MSG, 16), :], ones, (((0,), (0,)), ((), ())), preferred_element_type=F32
                )
                done = ((near_w[k, e] + far) / (near_t[k, e] + total)).astype(BF16)
                att[e, 0, pl.ds(k * QR, QR), :] = done[:QR]
                att[e, 1, pl.ds(k * QR, QR), :] = done[QR:]
        span = pl.ds(k0 * QR, nb * QR)
        mixed = jnp.concatenate([att[e, h, span, :] for e in range(2) for h in range(2)], axis=1)

        def columns(n, carry):
            at = pl.ds(pl.multiple_of(n * COLS, COLS), COLS)
            part[span, at] = jnp.dot(mixed, wo[:, at], preferred_element_type=F32).astype(BF16)
            return carry

        lax.fori_loop(0, STEPS, columns, 0)

    def add(dst, dst_rows, sources):
        def columns(n, carry):
            at = pl.ds(pl.multiple_of(n * COLS, COLS), COLS)
            total = dst[dst_rows, at].astype(F32)
            for ref, its in sources:
                total = total + ref[its, at].astype(F32)
            dst[dst_rows, at] = total.astype(BF16)
            return carry

        lax.fori_loop(0, STEPS, columns, 0)

    def t_copy(i, g, half):
        src = part.at[rows(g + 4, half)]
        return remote(src, rx.at[rows(g, half)], tx_s.at[i], tx_r.at[i], x_back)

    t_copies = [
        t_copy(0, 0, None), t_copy(1, 1, 1), t_copy(2, 2, 0),
        t_copy(3, 3, 0), t_copy(4, 3, 1), t_copy(5, 1, 0), t_copy(6, 2, 1),
    ]
    u_copies = [
        remote(part.at[rows(1, 1)], fin.at[0, pl.ds(HALF, HALF)], ty_s.at[0], ty_r.at[0], y_up),
        remote(part.at[rows(2, 0)], fin.at[1, pl.ds(0, HALF)], ty_s.at[1], ty_r.at[1], y_down),
        remote(part.at[rows(3, 0)], ry.at[pl.ds(0, HALF)], ty_s.at[2], ty_r.at[2], y_up),
        remote(part.at[rows(3, 1)], ry.at[pl.ds(HALF, HALF)], ty_s.at[3], ty_r.at[3], y_down),
        remote(part.at[rows(1, 0)], fin.at[0, pl.ds(0, HALF)], ty_s.at[4], ty_r.at[4], y_up),
        remote(part.at[rows(2, 1)], fin.at[1, pl.ds(HALF, HALF)], ty_s.at[5], ty_r.at[5], y_down),
    ]

    y_copies[0].wait_recv()
    x_copies[1].start()
    y_copies[4].start()
    y_copies[1].wait_recv()
    x_copies[2].start()
    y_copies[5].start()

    for i in range(3):
        local[i].wait()
    w_arrive(0, wq.at[1 - c])
    w_arrive(1, wkv.at[1 - c])
    handle(0, 1)
    x_copies[0].wait_recv()
    handle(4, 1)

    y_copies[2].wait_recv()
    x_copies[3].start()
    y_copies[3].wait_recv()
    x_copies[4].start()
    handle(1, 2)
    local[4].wait()
    local[5].wait()

    y_copies[4].wait_recv()
    x_copies[5].start()
    y_copies[5].wait_recv()
    x_copies[6].start()
    handle(3, 1)
    for i in range(1, 5):
        x_copies[i].wait_recv()
    handle(5, 2)
    x_copies[5].wait_recv()
    x_copies[6].wait_recv()
    handle(7, 1)

    source()

    w_arrive(2, wo.at[pl.ds(pl.multiple_of((1 - c) * 256, 256), 256)])
    project(5, 2)
    t_copies[1].start()
    t_copies[2].start()
    project(7, 1)
    for i in range(3, 7):
        t_copies[i].start()
    project(4, 1)
    t_copies[0].start()
    project(0, 4)

    t_copies[1].wait_recv()
    add(part, rows(1, 1), [(rx, rows(1, 1))])
    u_copies[0].start()
    t_copies[2].wait_recv()
    add(part, rows(2, 0), [(rx, rows(2, 0))])
    u_copies[1].start()
    t_copies[3].wait_recv()
    add(part, rows(3, 0), [(rx, rows(3, 0))])
    u_copies[2].start()
    t_copies[4].wait_recv()
    add(part, rows(3, 1), [(rx, rows(3, 1))])
    u_copies[3].start()
    t_copies[5].wait_recv()
    u_copies[2].wait_recv()
    add(part, rows(1, 0), [(rx, rows(1, 0)), (ry, pl.ds(0, HALF))])
    u_copies[4].start()
    t_copies[6].wait_recv()
    u_copies[3].wait_recv()
    add(part, rows(2, 1), [(rx, rows(2, 1)), (ry, pl.ds(HALF, HALF))])
    u_copies[5].start()
    t_copies[0].wait_recv()
    u_copies[0].wait_recv()
    u_copies[1].wait_recv()
    u_copies[4].wait_recv()
    u_copies[5].wait_recv()

    def finish(n, carry):
        at = pl.ds(pl.multiple_of(n * COLS, COLS), COLS)
        total = part[pl.ds(0, QR), at].astype(F32) + rx[pl.ds(0, QR), at].astype(F32)
        total = total + fin[0, :, at].astype(F32) + fin[1, :, at].astype(F32)
        out[:, at] = total.astype(BF16)
        return carry

    lax.fori_loop(0, STEPS, finish, 0)

    for copy in y_copies + x_copies + w_copies + t_copies + u_copies:
        copy.wait_send()

    for i in range(N):
        here, to, t = q_route(i // 2, i % 2)

        @pl.when(jnp.logical_not(here))
        def _():
            q_copy(i // 2, i % 2, to, t).wait_send()

        back_here, back_to = o_route(i)

        @pl.when(jnp.logical_not(back_here))
        def _():
            o_copy(i, back_to).wait_send()


def shards(tokens, w_query, w_keyval, w_out, kv_pool, req_target, page_counts, tail_tokens, migrate, pool_order):
    table = jnp.asarray(tables())
    anyspace = pl.BlockSpec(memory_space=pl.ANY)
    smem = pl.BlockSpec(memory_space=pltpu.SMEM)
    dma = pltpu.SemaphoreType.DMA
    return pl.pallas_call(
        kernel,
        out_shape=jax.ShapeDtypeStruct((QR, D), BF16),
        in_specs=[anyspace] * 5 + [smem] * 5 + [anyspace],
        out_specs=pl.BlockSpec(memory_space=pltpu.VMEM),
        scratch_shapes=[
            pltpu.VMEM((8 * QR, D), BF16),
            pltpu.VMEM((2, D, 256), BF16),
            pltpu.VMEM((2, D, 256), BF16),
            pltpu.VMEM((512, D), BF16),
            pltpu.VMEM((POOL, PAGE, 256), BF16),
            pltpu.VMEM((4 * QR + 8, HD), F32),
            pltpu.VMEM((8, 2, MSG, HD), BF16),
            pltpu.VMEM((N, MSG, HD), BF16),
            pltpu.VMEM((N, MSG, HD), BF16),
            pltpu.VMEM((8, 2, MSG, HD), F32),
            pltpu.VMEM((8, 2, MSG, HD), F32),
            pltpu.VMEM((POOL + 1, MSG, HD), F32),
            pltpu.VMEM((POOL + 1, MSG, HD), F32),
            pltpu.VMEM((N, OMSG, HD), BF16),
            pltpu.VMEM((8, 2, OMSG, HD), BF16),
            pltpu.VMEM((2, 2, 8 * QR, HD), BF16),
            pltpu.VMEM((8 * QR, D), BF16),
            pltpu.VMEM((4 * QR, D), BF16),
            pltpu.VMEM((QR, D), BF16),
            pltpu.VMEM((2, QR, D), BF16),
            pltpu.VMEM((N, 8, HD), F32),
            pltpu.VMEM((N, 8, HD), F32),
            pltpu.SMEM((N,), jnp.int32),
            pltpu.SMEM((N,), jnp.int32),
            pltpu.SMEM((N,), jnp.int32),
            dma((8,)),
            dma((3,)), dma((3,)),
            dma((6,)), dma((6,)),
            dma((7,)), dma((7,)),
            dma((N,)), dma((N,)),
            dma((N,)), dma((N,)),
            dma((7,)), dma((7,)),
            dma((6,)), dma((6,)),
        ],
        compiler_params=pltpu.CompilerParams(
            collective_id=0, has_side_effects=True, vmem_limit_bytes=58 * 2**20
        ),
        cost_estimate=pl.CostEstimate(flops=9 * 10**9, bytes_accessed=13 * 10**6, transcendentals=3 * 10**6),
    )(tokens, w_query, w_keyval, w_out, kv_pool, req_target, page_counts, tail_tokens, migrate, pool_order, table)


def solution(mesh):
    return jax.shard_map(
        shards,
        mesh=mesh,
        in_specs=(
            P(("inst", "tp"), None),
            P(None, "tp"),
            P(None, "tp"),
            P("tp", None),
            P("inst", None, "tp"),
            P("inst", None),
            P("inst", None),
            P("inst", None),
            P("inst", None),
            P("inst", None),
        ),
        out_specs=P(("inst", "tp"), None),
        check_vma=False,
    )
```
